32 devices in a mesh: rec: 4 (over y, x), ctx: 8 (over z, core).
Axes of the slice: x: 2, y: 2, z: 4, core: 2. Of those that a mesh axis runs over, the one named last changes fastest.
Arguments:
- queries: bfloat16 [4, 256, 2048], P('rec', 'ctx'), may hold values from -360 to 360
- grad_out: bfloat16 [4, 256, 2048], P('rec', 'ctx'), may hold values from -6 to 6
- keys: bfloat16 [1024, 2048], P('ctx'), may hold values from -13 to 13
- values: bfloat16 [1024, 2048], P('ctx'), may hold values from -6 to 6
- surv_index: int32 [4, 256], P('rec'), may hold values from 0 to 127, as said below
- counts: int32 [4, 8], P('rec'), may hold values from 1 to 32, as said below
Outputs:
- query_grad: bfloat16 [4, 256, 2048], P('rec', 'ctx')
- key_grad: bfloat16 [1024, 2048], P('ctx', 'rec')
- value_grad: bfloat16 [1024, 2048], P('ctx', 'rec')
The draws below stay inside these ranges and needn't reach their ends.
Inputs may be any that keep to these rules, and one draw needn't show every extreme that they name: `surv_index`: in each depth and index of ctx the live slots come first and hold distinct positions in increasing order; the other slots hold 0. In each depth and index of ctx whose 32 slots are all live, one live slot holds position 127. `counts`: in every depth some index of ctx has all 32 slots live.
All inputs are finite; a program needn't handle non-finite values.
Results may differ from the reference program's by a relative error of at most 0.0051.
Values may be sent and summed in bfloat16 or wider, within the bound.
A program may use at most 64 MiB of HBM per device.

```python
import math
import jax
import jax.numpy as jnp
from jax import lax

HEADS = 16
HEAD_DIM = 128
TOK_DEV = 128
CAP = 32
DEPTHS = 4
TOKENS = 1024
CAPS = 256
HD = 2048
N_CTX = 8


def key_rows(random_seed_key):
    normals = jax.random.normal(jax.random.fold_in(random_seed_key, 11), (TOKENS, HEADS * HEAD_DIM), jnp.float32)
    normals = jnp.clip(normals, -6.0, 6.0)
    return normals


def draw_keys(key, part):
    return key_rows(key).astype(jnp.bfloat16)


def draw_queries(key, part):
    slot_total = CAP * N_CTX
    normals = jax.random.normal(jax.random.fold_in(key, 21), (DEPTHS, slot_total, HEADS * HEAD_DIM), jnp.float32)
    normals = jnp.clip(normals, -6.0, 6.0)
    return normals.astype(jnp.bfloat16)


def remaining_token_counts(random_seed_key):
    drawn = jax.random.randint(jax.random.fold_in(random_seed_key, 31), (DEPTHS, N_CTX), 1, CAP + 1)
    fullest = jax.random.randint(jax.random.fold_in(random_seed_key, 32), (DEPTHS, 1), 0, N_CTX)
    return jnp.where(jnp.arange(N_CTX)[None, :] == fullest, CAP, drawn).astype(jnp.int32)


def draw_counts(key, part):
    return remaining_token_counts(key)


def draw_surv_index(key, part):
    active_count_list = remaining_token_counts(key)
    rank_keys = jax.random.randint(jax.random.fold_in(key, 33), (DEPTHS, N_CTX, TOK_DEV), 0, 2 ** 18)
    rank_keys = rank_keys * TOK_DEV + jnp.arange(TOK_DEV)[None, None, :]
    lastpos = jnp.arange(TOK_DEV) == TOK_DEV - 1
    rank_keys = jnp.where(lastpos[None, None, :] & (active_count_list[:, :, None] == CAP), -1, rank_keys)
    ordering = jnp.argsort(rank_keys, axis=-1).astype(jnp.int32)
    chosen = ordering[:, :, :CAP]
    is_live = jnp.arange(CAP)[None, None, :] < active_count_list[:, :, None]
    marked = jnp.where(is_live, chosen, TOK_DEV)
    ordered = jnp.sort(marked, axis=-1)
    indices = jnp.where(ordered == TOK_DEV, 0, ordered)
    return indices.reshape(DEPTHS, N_CTX * CAP).astype(jnp.int32)


def block_levels(key, shape, shards, smallest, top_value):
    gain, own = 1.0, jax.random.fold_in(key, 6)
    for position, shards_of in shards:
        heights = jnp.exp(jax.random.uniform(jax.random.fold_in(own, position), (shards_of,), jnp.float32, smallest / len(shards), top_value / len(shards)))
        gain = gain * jnp.repeat(heights, shape[position] // shards_of).reshape([-1 if axis == position else 1 for axis in range(len(shape))])
    return gain


def bell_draw(key, extent, scale, reach, pieces=(), kind=jnp.bfloat16):
    array = jax.random.normal(key, extent, jnp.float32) * scale
    if len(pieces) > 0:
        array = block_levels(key, extent, pieces, -0.22, 0.18) * array
    return jnp.clip(array, min=-reach, max=reach).astype(kind)


def setup_inputs(seed: int = 0) -> dict:
    streams_of = jax.random.split(jax.random.key(seed), 7)
    return {
        "queries": draw_queries(jax.random.fold_in(streams_of[6], 71), 0),
        "grad_out": bell_draw(streams_of[1], (DEPTHS, CAPS, HD), 1.0, 6.0, ((0, 4), (1, 8))),
        "keys": draw_keys(jax.random.fold_in(streams_of[6], 71), 0),
        "values": bell_draw(streams_of[3], (TOKENS, HD), 1.0, 6.0, ((0, 8),)),
        "surv_index": draw_surv_index(jax.random.fold_in(streams_of[6], 71), 0),
        "counts": draw_counts(jax.random.fold_in(streams_of[6], 71), 0),
    }


def rounded(array_in):
    return lax.optimization_barrier(array_in.astype(jnp.bfloat16)).astype(jnp.float32)

def depth_backward(depth_queries, depth_grads, surv_row, count_row, keys_split, value_pieces):
    slot_ids = jnp.arange(CAP * N_CTX)
    key_pos = jnp.arange(TOKENS)
    query_pos = slot_ids // CAP * TOK_DEV + surv_row
    is_live = slot_ids % CAP < jnp.repeat(count_row, CAP)
    visible = key_pos[None, :] <= query_pos[:, None]
    factor = 1.0 / math.sqrt(HEAD_DIM)
    query_split = depth_queries.astype(jnp.float32).reshape(CAP * N_CTX, HEADS, HEAD_DIM).transpose(1, 0, 2)
    masked_grads = jnp.where(is_live[:, None], depth_grads.astype(jnp.float32), 0.0)
    grad_split = masked_grads.reshape(CAP * N_CTX, HEADS, HEAD_DIM).transpose(1, 0, 2)

    def per_head(operands):
        query_head, grad_head, key_head, value_head = operands
        score_matrix = factor * jnp.dot(query_head, key_head.T, precision=lax.Precision.HIGHEST)
        row_max = lax.optimization_barrier(jnp.max(jnp.where(visible, score_matrix, -jnp.inf), axis=1))
        row_sum = lax.optimization_barrier(jnp.sum(jnp.where(visible, jnp.exp(score_matrix - row_max[:, None]), 0.0), axis=1))
        log_total = row_max + jnp.log(row_sum)
        weights = jnp.where(visible, jnp.exp(score_matrix - log_total[:, None]), 0.0)
        grad_weights = jnp.dot(grad_head, value_head.T, precision=lax.Precision.HIGHEST)
        row_delta = lax.optimization_barrier(jnp.sum(weights * grad_weights, axis=1))
        grad_scores = rounded(weights * (grad_weights - row_delta[:, None]))
        low_weights = rounded(weights)
        query_term = factor * jnp.dot(grad_scores, key_head, precision=lax.Precision.HIGHEST)
        key_term = factor * jnp.dot(grad_scores.T, query_head, precision=lax.Precision.HIGHEST)
        value_term = jnp.dot(low_weights.T, grad_head, precision=lax.Precision.HIGHEST)
        return (query_term, key_term, value_term)
    return lax.map(per_head, (query_split, grad_split, keys_split, value_pieces))

def reference(queries, grad_out, keys, values, surv_index, counts):
    keys_split = keys.astype(jnp.float32).reshape(TOKENS, HEADS, HEAD_DIM).transpose(1, 0, 2)
    value_pieces = values.astype(jnp.float32).reshape(TOKENS, HEADS, HEAD_DIM).transpose(1, 0, 2)

    def per_depth(totals, operands):
        depth_queries, depth_grads, surv_row, count_row = operands
        query_term, key_term, value_term = depth_backward(depth_queries, depth_grads, surv_row, count_row, keys_split, value_pieces)
        return ((totals[0] + key_term, totals[1] + value_term), query_term)
    empty_sum = jnp.zeros((HEADS, TOKENS, HEAD_DIM), jnp.float32)
    sums, query_terms = lax.scan(per_depth, (empty_sum, empty_sum), (queries, grad_out, surv_index, counts))
    query_grad = query_terms.transpose(0, 2, 1, 3).reshape(DEPTHS, CAP * N_CTX, HEADS * HEAD_DIM).astype(jnp.bfloat16)
    key_grad = sums[0].transpose(1, 0, 2).reshape(TOKENS, HEADS * HEAD_DIM).astype(jnp.bfloat16)
    value_grad = sums[1].transpose(1, 0, 2).reshape(TOKENS, HEADS * HEAD_DIM).astype(jnp.bfloat16)
    return (query_grad, key_grad, value_grad)
```

```python
import functools
import math

import jax
import jax.numpy as jnp
from jax import lax
from jax.experimental import pallas as pl
from jax.experimental.pallas import tpu as pltpu
from jax.sharding import PartitionSpec as P

HEADS = 16
HEAD_DIM = 128
NEG_FILL = -1e30
MESH = pl.DeviceIdType.MESH
NT = (((1,), (1,)), ((), ()))
TN = (((0,), (0,)), ((), ()))


def kernel(
    recs, ctxs, q_ref, g_ref, k_ref, v_ref, surv_ref, counts_ref,
    dq_ref, dk_ref, dv_ref,
    pos, qg, kv, acc, peer, dq_buf, dkv_buf,
    pos_send, pos_recv, qg_send, qg_recv, kv_send, kv_recv, fwd_send,
    acc_send, acc_recv, dq_send, dq_recv, dkv_send, dkv_recv,
):
    groups = HEADS // recs
    parts = ctxs // groups
    cap = q_ref.shape[1]
    tok = k_ref.shape[0]
    slots = recs * cap
    r = lax.axis_index("rec")
    c = lax.axis_index("ctx")
    z = c // parts
    part = c % parts
    factor = 1.0 / math.sqrt(HEAD_DIM)

    def head_cols(rec, group):
        return pl.ds(pl.multiple_of((rec * groups + group) * HEAD_DIM, HEAD_DIM), HEAD_DIM)

    others = [(dr, dz) for dz in range(groups) for dr in range(recs) if dr or dz]

    def partner(dr, dz):
        return (lax.rem(r + dr, recs), lax.rem(z + dz, groups))

    def sibling(dp):
        return lax.rem(part + dp, parts)

    barrier = pltpu.get_barrier_semaphore()
    for dr, dz in others:
        pr, pz = partner(dr, dz)
        pl.semaphore_signal(barrier, inc=1, device_id=(pr, pz * parts + part), device_id_type=MESH)
    for dp in range(1, parts):
        pl.semaphore_signal(
            barrier, inc=1, device_id=(r, z * parts + sibling(dp)), device_id_type=MESH
        )

    row = jnp.broadcast_to(surv_ref[...], (8, surv_ref.shape[1]))
    lane = lax.broadcasted_iota(jnp.int32, (1, slots), 1)
    here = lane - r * cap
    for zs in range(groups):
        cs = zs * parts + part
        moved = pltpu.roll(row, lax.rem(r * cap - cs * cap + ctxs * cap, ctxs * cap), 1)
        live = (here >= 0) & (here < cap) & (here < counts_ref[0, cs])
        pos[r, zs : zs + 1, :] = jnp.where(live, moved[0:1, 0:slots] + cs * tok + 1, 0)

    mine = []
    rows_r = pl.ds(pl.multiple_of(r * cap, cap), cap)
    for i, ref in enumerate((q_ref, g_ref)):
        mine.append(pltpu.make_async_copy(
            ref.at[0, :, head_cols(r, z)], qg.at[z, i, rows_r, :], qg_recv.at[z]))
    for i, ref in enumerate((k_ref, v_ref)):
        mine.append(pltpu.make_async_copy(ref.at[:, head_cols(r, z)], kv.at[c, i], kv_recv.at[c]))
    for copy in mine:
        copy.start()

    pl.semaphore_wait(barrier, len(others) + parts - 1)

    sends = []

    def send(src, dst, send_sem, recv_sem, device):
        copy = pltpu.make_async_remote_copy(
            src_ref=src, dst_ref=dst, send_sem=send_sem, recv_sem=recv_sem,
            device_id=device, device_id_type=MESH,
        )
        copy.start()
        sends.append(copy)

    for dz in range(1, groups):
        pz = lax.rem(z + dz, groups)
        for i, ref in enumerate((k_ref, v_ref)):
            send(ref.at[:, head_cols(r, pz)], kv.at[c, i], kv_send.at[dz, i], kv_recv.at[c],
                 (r, pz * parts + part))
    for dr in range(1, recs):
        send(pos.at[r], pos.at[r], pos_send.at[dr], pos_recv.at[r], (lax.rem(r + dr, recs), c))
    for dr, dz in others:
        pr, pz = partner(dr, dz)
        for i, ref in enumerate((q_ref, g_ref)):
            send(ref.at[0, :, head_cols(pr, pz)], qg.at[z, i, rows_r, :],
                 qg_send.at[dz, dr, i], qg_recv.at[z], (pr, pz * parts + part))
    for dp in range(1, parts):
        for i, ref in enumerate((k_ref, v_ref)):
            send(ref.at[:, head_cols(r, z)], kv.at[c, i], fwd_send.at[dp, 0, i], kv_recv.at[c],
                 (r, z * parts + sibling(dp)))

    def arrived(ref, sem):
        pltpu.make_async_copy(ref, ref, sem).wait()

    for dz in range(1, groups):
        cs = lax.rem(z + dz, groups) * parts + part
        arrived(kv.at[cs], kv_recv.at[cs])
        for dp in range(1, parts):
            send(kv.at[cs], kv.at[cs], fwd_send.at[dp, dz, 0], kv_recv.at[cs],
                 (r, z * parts + sibling(dp)))
    arrived(kv.at[c], kv_recv.at[c])
    for dr in range(1, recs):
        rs = lax.rem(r + dr, recs)
        arrived(pos.at[rs], pos_recv.at[rs])
    for dz in range(groups):
        for dp in range(1, parts):
            cs = lax.rem(z + dz, groups) * parts + sibling(dp)
            arrived(kv.at[cs], kv_recv.at[cs])

    place = sum(pos[rs] for rs in range(recs)) - 1

    for zs in reversed(range(groups)):
        blocks = (zs + 1) * parts
        length = blocks * tok
        arrived(qg.at[zs], qg_recv.at[zs])
        q, g = qg[zs, 0], qg[zs, 1]
        keys = kv[0:blocks, 0].reshape(length, HEAD_DIM)
        vals = kv[0:blocks, 1].reshape(length, HEAD_DIM)
        scores = lax.dot_general(keys, q, NT, preferred_element_type=jnp.float32)
        seen = lax.broadcasted_iota(jnp.int32, (length, slots), 0) <= place[zs : zs + 1, :]
        scores = jnp.where(seen, scores * (factor * math.log2(math.e)), NEG_FILL)
        top = jnp.maximum(jnp.max(scores, axis=0, keepdims=True), 0.1 * NEG_FILL)
        raw = jnp.exp2(scores - top)
        total = jnp.sum(raw, axis=0, keepdims=True)
        weights = raw * (1.0 / jnp.maximum(total, 1e-30))
        grads = lax.dot_general(vals, g, NT, preferred_element_type=jnp.float32)
        delta = jnp.sum(weights * grads, axis=0, keepdims=True)
        ds = (weights * (grads - delta)).astype(jnp.bfloat16)
        wb = weights.astype(jnp.bfloat16)
        dq = lax.dot_general(ds, keys, TN, preferred_element_type=jnp.float32)
        dq_buf[zs] = (dq * factor).astype(jnp.bfloat16)
        for rd in range(recs):
            src = dq_buf.at[zs, rd * cap : (rd + 1) * cap, :]
            dst = dq_ref.at[0, :, head_cols(r, z)]
            home = (r == rd) & (z == zs)

            @pl.when(home)
            def _():
                pltpu.make_async_copy(src, dst, dq_recv).start()

            @pl.when(jnp.logical_not(home))
            def _():
                pltpu.make_async_remote_copy(
                    src_ref=src, dst_ref=dst, send_sem=dq_send.at[zs, rd], recv_sem=dq_recv,
                    device_id=(rd, zs * parts + part), device_id_type=MESH,
                ).start()

        dk = lax.dot_general(ds, q, (((1,), (0,)), ((), ())), preferred_element_type=jnp.float32)
        dv = lax.dot_general(wb, g, (((1,), (0,)), ((), ())), preferred_element_type=jnp.float32)
        dk = dk.reshape(blocks, tok, HEAD_DIM)
        dv = dv.reshape(blocks, tok, HEAD_DIM)
        if zs == groups - 1:
            acc[0:blocks, 0] = dk
            acc[0:blocks, 1] = dv
        else:
            acc[0:blocks, 0] += dk
            acc[0:blocks, 1] += dv
        for dp in range(1, parts):
            cd = zs * parts + sibling(dp)
            send(acc.at[cd], peer.at[parts - dp, zs], acc_send.at[dp, zs],
                 acc_recv.at[parts - dp, zs], (r, z * parts + sibling(dp)))

    for zs in reversed(range(groups)):
        dkv = acc[zs * parts + part]
        for dp in range(1, parts):
            arrived(peer.at[dp, zs], acc_recv.at[dp, zs])
            dkv += peer[dp, zs]
        dkv_buf[zs, 0] = (dkv[0] * factor).astype(jnp.bfloat16)
        dkv_buf[zs, 1] = dkv[1].astype(jnp.bfloat16)
        cols = pl.ds(pl.multiple_of(z * HEAD_DIM, HEAD_DIM), HEAD_DIM)
        for i, ref in enumerate((dk_ref, dv_ref)):

            @pl.when(z == zs)
            def _():
                pltpu.make_async_copy(dkv_buf.at[zs, i], ref.at[:, cols], dkv_recv.at[i]).start()

            @pl.when(z != zs)
            def _():
                pltpu.make_async_remote_copy(
                    src_ref=dkv_buf.at[zs, i], dst_ref=ref.at[:, cols],
                    send_sem=dkv_send.at[zs, i], recv_sem=dkv_recv.at[i],
                    device_id=(r, zs * parts + part), device_id_type=MESH,
                ).start()

    for copy in sends:
        copy.wait_send()
    for zs in range(groups):
        for rd in range(recs):

            @pl.when(jnp.logical_not((r == rd) & (z == zs)))
            def _():
                arrived(dq_buf.at[zs, rd * cap : (rd + 1) * cap, :], dq_send.at[zs, rd])

        for i in range(2):

            @pl.when(z != zs)
            def _():
                arrived(dkv_buf.at[zs, i], dkv_send.at[zs, i])

    arrived(dq_ref, dq_recv)
    arrived(dk_ref, dkv_recv.at[0])
    arrived(dv_ref, dkv_recv.at[1])


def body(queries, grad_out, keys, values, surv_index, counts):
    recs = lax.axis_size("rec")
    ctxs = lax.axis_size("ctx")
    cap, tok = queries.shape[1], keys.shape[0]
    groups = HEADS // recs
    parts = ctxs // groups
    slots = recs * cap
    dma = pltpu.SemaphoreType.DMA
    anywhere = pl.BlockSpec(memory_space=pl.ANY)
    return pl.pallas_call(
        functools.partial(kernel, recs, ctxs),
        out_shape=(
            jax.ShapeDtypeStruct(queries.shape, jnp.bfloat16),
            jax.ShapeDtypeStruct((tok, groups * HEAD_DIM), jnp.bfloat16),
            jax.ShapeDtypeStruct((tok, groups * HEAD_DIM), jnp.bfloat16),
        ),
        in_specs=[anywhere] * 4 + [
            pl.BlockSpec(memory_space=pltpu.VMEM),
            pl.BlockSpec(memory_space=pltpu.SMEM),
        ],
        out_specs=(anywhere,) * 3,
        scratch_shapes=[
            pltpu.VMEM((recs, 8, slots), jnp.int32),
            pltpu.VMEM((groups, 2, slots, HEAD_DIM), jnp.bfloat16),
            pltpu.VMEM((ctxs, 2, tok, HEAD_DIM), jnp.bfloat16),
            pltpu.VMEM((ctxs, 2, tok, HEAD_DIM), jnp.float32),
            pltpu.VMEM((parts, groups, 2, tok, HEAD_DIM), jnp.float32),
            pltpu.VMEM((groups, slots, HEAD_DIM), jnp.bfloat16),
            pltpu.VMEM((groups, 2, tok, HEAD_DIM), jnp.bfloat16),
            dma((recs,)), dma((recs,)),
            dma((groups, recs, 2)), dma((groups,)),
            dma((groups, 2)), dma((ctxs,)),
            dma((parts, groups, 2)),
            dma((parts, groups)), dma((parts, groups)),
            dma((groups, recs)), dma,
            dma((groups, 2)), dma((2,)),
        ],
        compiler_params=pltpu.CompilerParams(
            collective_id=0, has_side_effects=True, vmem_limit_bytes=48 * 2**20
        ),
        cost_estimate=pl.CostEstimate(
            flops=10 * groups * slots * ctxs * tok * HEAD_DIM,
            bytes_accessed=4 * ctxs * tok * HEAD_DIM * 2,
            transcendentals=groups * slots * ctxs * tok,
        ),
    )(queries, grad_out, keys, values, surv_index, counts)


def solution(mesh):
    in_specs = (
        P("rec", "ctx", None),
        P("rec", "ctx", None),
        P("ctx", None),
        P("ctx", None),
        P("rec", None),
        P("rec", None),
    )
    out_specs = (P("rec", "ctx", None), P("ctx", "rec"), P("ctx", "rec"))
    return jax.shard_map(body, mesh=mesh, in_specs=in_specs, out_specs=out_specs, check_vma=False)
```

```python
import functools
import math

import jax
import jax.numpy as jnp
from jax import lax
from jax.experimental import pallas as pl
from jax.experimental.pallas import tpu as pltpu
from jax.sharding import PartitionSpec as P

HEADS = 16
HEAD_DIM = 128
NEG_FILL = -1e30
MESH = pl.DeviceIdType.MESH
NT = (((1,), (1,)), ((), ()))
TN = (((0,), (0,)), ((), ()))


def kernel(
    recs, ctxs, q_ref, g_ref, k_ref, v_ref, surv_ref, counts_ref,
    dq_ref, dk_ref, dv_ref,
    surv, live_counts, pos, qg, kv, acc, peer, dq_buf, dkv_buf,
    int_sem, pos_send, pos_recv, qg_send, qg_recv, kv_send, kv_recv, fwd_send,
    acc_send, acc_recv, dq_send, dq_recv, dkv_send, dkv_recv,
):
    groups = HEADS // recs
    parts = ctxs // groups
    cap = q_ref.shape[1]
    tok = k_ref.shape[0]
    slots = recs * cap
    r = lax.axis_index("rec")
    c = lax.axis_index("ctx")
    z = c // parts
    part = c % parts
    factor = 1.0 / math.sqrt(HEAD_DIM)

    def head_cols(rec, group):
        return pl.ds(pl.multiple_of((rec * groups + group) * HEAD_DIM, HEAD_DIM), HEAD_DIM)

    others = [(dr, dz) for dz in range(groups) for dr in range(recs) if dr or dz]

    def partner(dr, dz):
        return (lax.rem(r + dr, recs), lax.rem(z + dz, groups))

    def sibling(dp):
        return lax.rem(part + dp, parts)

    ints = [
        pltpu.make_async_copy(surv_ref, surv, int_sem.at[0]),
        pltpu.make_async_copy(counts_ref, live_counts, int_sem.at[1]),
    ]
    for copy in ints:
        copy.start()

    barrier = pltpu.get_barrier_semaphore()
    for dr, dz in others:
        pr, pz = partner(dr, dz)
        pl.semaphore_signal(barrier, inc=1, device_id=(pr, pz * parts + part), device_id_type=MESH)
    for dp in range(1, parts):
        pl.semaphore_signal(
            barrier, inc=1, device_id=(r, z * parts + sibling(dp)), device_id_type=MESH
        )

    mine = []
    rows_r = pl.ds(pl.multiple_of(r * cap, cap), cap)
    for i, ref in enumerate((q_ref, g_ref)):
        mine.append(pltpu.make_async_copy(
            ref.at[0, :, head_cols(r, z)], qg.at[z, i, rows_r, :], qg_recv.at[z]))
    for i, ref in enumerate((k_ref, v_ref)):
        mine.append(pltpu.make_async_copy(ref.at[:, head_cols(r, z)], kv.at[c, i], kv_recv.at[c]))
    for copy in mine:
        copy.start()

    for copy in ints:
        copy.wait()
    row = jnp.broadcast_to(surv[...], (8, surv.shape[1]))
    lane = lax.broadcasted_iota(jnp.int32, (1, slots), 1)
    here = lane - r * cap
    for zs in range(groups):
        cs = zs * parts + part
        moved = pltpu.roll(row, lax.rem(r * cap - cs * cap + ctxs * cap, ctxs * cap), 1)
        live = (here >= 0) & (here < cap) & (here < live_counts[0, cs])
        pos[r, zs : zs + 1, :] = jnp.where(live, moved[0:1, 0:slots] + cs * tok + 1, 0)

    pl.semaphore_wait(barrier, len(others) + parts - 1)

    sends = []

    def send(src, dst, send_sem, recv_sem, device):
        copy = pltpu.make_async_remote_copy(
            src_ref=src, dst_ref=dst, send_sem=send_sem, recv_sem=recv_sem,
            device_id=device, device_id_type=MESH,
        )
        copy.start()
        sends.append(copy)

    for dz in range(1, groups):
        pz = lax.rem(z + dz, groups)
        for i, ref in enumerate((k_ref, v_ref)):
            send(ref.at[:, head_cols(r, pz)], kv.at[c, i], kv_send.at[dz, i], kv_recv.at[c],
                 (r, pz * parts + part))
    for dr in range(1, recs):
        send(pos.at[r], pos.at[r], pos_send.at[dr], pos_recv.at[r], (lax.rem(r + dr, recs), c))
    for dr, dz in others:
        pr, pz = partner(dr, dz)
        for i, ref in enumerate((q_ref, g_ref)):
            send(ref.at[0, :, head_cols(pr, pz)], qg.at[z, i, rows_r, :],
                 qg_send.at[dz, dr, i], qg_recv.at[z], (pr, pz * parts + part))
    for dp in range(1, parts):
        for i, ref in enumerate((k_ref, v_ref)):
            send(ref.at[:, head_cols(r, z)], kv.at[c, i], fwd_send.at[dp, 0, i], kv_recv.at[c],
                 (r, z * parts + sibling(dp)))

    def arrived(ref, sem):
        pltpu.make_async_copy(ref, ref, sem).wait()

    for dz in range(1, groups):
        cs = lax.rem(z + dz, groups) * parts + part
        arrived(kv.at[cs], kv_recv.at[cs])
        for dp in range(1, parts):
            send(kv.at[cs], kv.at[cs], fwd_send.at[dp, dz, 0], kv_recv.at[cs],
                 (r, z * parts + sibling(dp)))
    arrived(kv.at[c], kv_recv.at[c])
    for dr in range(1, recs):
        rs = lax.rem(r + dr, recs)
        arrived(pos.at[rs], pos_recv.at[rs])
    for dz in range(groups):
        for dp in range(1, parts):
            cs = lax.rem(z + dz, groups) * parts + sibling(dp)
            arrived(kv.at[cs], kv_recv.at[cs])

    place = sum(pos[rs] for rs in range(recs)) - 1

    def finish(zs):
        dkv = acc[zs * parts + part]
        for dp in range(1, parts):
            arrived(peer.at[dp, zs], acc_recv.at[dp, zs])
            dkv += peer[dp, zs]
        dkv_buf[zs, 0] = (dkv[0] * factor).astype(jnp.bfloat16)
        dkv_buf[zs, 1] = dkv[1].astype(jnp.bfloat16)
        cols = pl.ds(pl.multiple_of(z * HEAD_DIM, HEAD_DIM), HEAD_DIM)
        for i, ref in enumerate((dk_ref, dv_ref)):

            @pl.when(z == zs)
            def _():
                pltpu.make_async_copy(dkv_buf.at[zs, i], ref.at[:, cols], dkv_recv.at[i]).start()

            @pl.when(z != zs)
            def _():
                pltpu.make_async_remote_copy(
                    src_ref=dkv_buf.at[zs, i], dst_ref=ref.at[:, cols],
                    send_sem=dkv_send.at[zs, i], recv_sem=dkv_recv.at[i],
                    device_id=(r, zs * parts + part), device_id_type=MESH,
                ).start()

    for zs in reversed(range(groups)):
        blocks = (zs + 1) * parts
        length = blocks * tok
        arrived(qg.at[zs], qg_recv.at[zs])
        q, g = qg[zs, 0], qg[zs, 1]
        keys = kv[0:blocks, 0].reshape(length, HEAD_DIM)
        vals = kv[0:blocks, 1].reshape(length, HEAD_DIM)
        scores = lax.dot_general(keys, q, NT, preferred_element_type=jnp.float32)
        seen = lax.broadcasted_iota(jnp.int32, (length, slots), 0) <= place[zs : zs + 1, :]
        scores = jnp.where(seen, scores * (factor * math.log2(math.e)), NEG_FILL)
        top = jnp.maximum(jnp.max(scores, axis=0, keepdims=True), 0.1 * NEG_FILL)
        raw = jnp.exp2(scores - top)
        total = jnp.sum(raw, axis=0, keepdims=True)
        weights = raw * (1.0 / jnp.maximum(total, 1e-30))
        grads = lax.dot_general(vals, g, NT, preferred_element_type=jnp.float32)
        delta = jnp.sum(weights * grads, axis=0, keepdims=True)
        ds = (weights * (grads - delta)).astype(jnp.bfloat16)
        wb = weights.astype(jnp.bfloat16)
        dq = lax.dot_general(ds, keys, TN, preferred_element_type=jnp.float32)
        dq_buf[zs] = (dq * factor).astype(jnp.bfloat16)
        for rd in range(recs):
            src = dq_buf.at[zs, rd * cap : (rd + 1) * cap, :]
            dst = dq_ref.at[0, :, head_cols(r, z)]
            home = (r == rd) & (z == zs)

            @pl.when(home)
            def _():
                pltpu.make_async_copy(src, dst, dq_recv).start()

            @pl.when(jnp.logical_not(home))
            def _():
                pltpu.make_async_remote_copy(
                    src_ref=src, dst_ref=dst, send_sem=dq_send.at[zs, rd], recv_sem=dq_recv,
                    device_id=(rd, zs * parts + part), device_id_type=MESH,
                ).start()

        dk = lax.dot_general(ds, q, (((1,), (0,)), ((), ())), preferred_element_type=jnp.float32)
        dv = lax.dot_general(wb, g, (((1,), (0,)), ((), ())), preferred_element_type=jnp.float32)
        dk = dk.reshape(blocks, tok, HEAD_DIM)
        dv = dv.reshape(blocks, tok, HEAD_DIM)
        if zs == groups - 1:
            acc[0:blocks, 0] = dk
            acc[0:blocks, 1] = dv
        else:
            acc[0:blocks, 0] += dk
            acc[0:blocks, 1] += dv
        for dp in range(1, parts):
            cd = zs * parts + sibling(dp)
            send(acc.at[cd], peer.at[parts - dp, zs], acc_send.at[dp, zs],
                 acc_recv.at[parts - dp, zs], (r, z * parts + sibling(dp)))
        if zs < groups - 1:
            finish(zs + 1)
    finish(0)


    for copy in sends:
        copy.wait_send()
    for zs in range(groups):
        for rd in range(recs):

            @pl.when(jnp.logical_not((r == rd) & (z == zs)))
            def _():
                arrived(dq_buf.at[zs, rd * cap : (rd + 1) * cap, :], dq_send.at[zs, rd])

        for i in range(2):

            @pl.when(z != zs)
            def _():
                arrived(dkv_buf.at[zs, i], dkv_send.at[zs, i])

    arrived(dq_ref, dq_recv)
    arrived(dk_ref, dkv_recv.at[0])
    arrived(dv_ref, dkv_recv.at[1])


def hand_over(a, b, c, a_out, b_out, c_out, sem):
    copies = [
        pltpu.make_async_copy(src, dst, sem.at[i])
        for i, (src, dst) in enumerate(((a, a_out), (b, b_out), (c, c_out)))
    ]
    for copy in copies:
        copy.start()
    for copy in copies:
        copy.wait()


def body(queries, grad_out, keys, values, surv_index, counts):
    recs = lax.axis_size("rec")
    ctxs = lax.axis_size("ctx")
    cap, tok = queries.shape[1], keys.shape[0]
    groups = HEADS // recs
    parts = ctxs // groups
    slots = recs * cap
    dma = pltpu.SemaphoreType.DMA
    anywhere = pl.BlockSpec(memory_space=pltpu.HBM)
    results = pl.pallas_call(
        functools.partial(kernel, recs, ctxs),
        out_shape=(
            jax.ShapeDtypeStruct(queries.shape, jnp.bfloat16),
            jax.ShapeDtypeStruct((tok, groups * HEAD_DIM), jnp.bfloat16),
            jax.ShapeDtypeStruct((tok, groups * HEAD_DIM), jnp.bfloat16),
        ),
        in_specs=[anywhere] * 6,
        out_specs=(anywhere,) * 3,
        scratch_shapes=[
            pltpu.VMEM(surv_index.shape, jnp.int32),
            pltpu.SMEM(counts.shape, jnp.int32),
            pltpu.VMEM((recs, 8, slots), jnp.int32),
            pltpu.VMEM((groups, 2, slots, HEAD_DIM), jnp.bfloat16),
            pltpu.VMEM((ctxs, 2, tok, HEAD_DIM), jnp.bfloat16),
            pltpu.VMEM((ctxs, 2, tok, HEAD_DIM), jnp.float32),
            pltpu.VMEM((parts, groups, 2, tok, HEAD_DIM), jnp.float32),
            pltpu.VMEM((groups, slots, HEAD_DIM), jnp.bfloat16),
            pltpu.VMEM((groups, 2, tok, HEAD_DIM), jnp.bfloat16),
            dma((2,)), dma((recs,)), dma((recs,)),
            dma((groups, recs, 2)), dma((groups,)),
            dma((groups, 2)), dma((ctxs,)),
            dma((parts, groups, 2)),
            dma((parts, groups)), dma((parts, groups)),
            dma((groups, recs)), dma,
            dma((groups, 2)), dma((2,)),
        ],
        compiler_params=pltpu.CompilerParams(
            collective_id=0, has_side_effects=True, vmem_limit_bytes=64 * 2**20
        ),
        cost_estimate=pl.CostEstimate(
            flops=10 * groups * slots * ctxs * tok * HEAD_DIM,
            bytes_accessed=4 * ctxs * tok * HEAD_DIM * 2,
            transcendentals=groups * slots * ctxs * tok,
        ),
    )(queries, grad_out, keys, values, surv_index, counts)
    return pl.pallas_call(
        hand_over,
        out_shape=tuple(jax.ShapeDtypeStruct(a.shape, a.dtype) for a in results),
        in_specs=[anywhere] * 3,
        out_specs=(anywhere,) * 3,
        scratch_shapes=[dma((3,))],
        compiler_params=pltpu.CompilerParams(vmem_limit_bytes=64 * 2**20),
    )(*results)


def solution(mesh):
    in_specs = (
        P("rec", "ctx", None),
        P("rec", "ctx", None),
        P("ctx", None),
        P("ctx", None),
        P("rec", None),
        P("rec", None),
    )
    out_specs = (P("rec", "ctx", None), P("ctx", "rec"), P("ctx", "rec"))
    return jax.shard_map(body, mesh=mesh, in_specs=in_specs, out_specs=out_specs, check_vma=False)
```

```python
import functools
import math

import jax
import jax.numpy as jnp
from jax import lax
from jax.experimental import pallas as pl
from jax.experimental.pallas import tpu as pltpu
from jax.sharding import PartitionSpec as P

HEADS = 16
HEAD_DIM = 128
NEG_FILL = -1e30
MESH = pl.DeviceIdType.MESH
NT = (((1,), (1,)), ((), ()))
TN = (((0,), (0,)), ((), ()))


def kernel(
    recs, ctxs, q_ref, g_ref, k_ref, v_ref, surv_ref, counts_ref,
    dq_ref, dk_ref, dv_ref,
    surv, live_counts, pos, qg, kv, acc, peer, dq_buf, dkv_buf,
    int_sem, pos_send, pos_recv, qg_send, qg_recv, kv_send, kv_recv, fwd_send,
    acc_send, acc_recv, dq_send, dq_recv, dkv_send, dkv_recv,
):
    groups = HEADS // recs
    parts = ctxs // groups
    cap = q_ref.shape[1]
    tok = k_ref.shape[0]
    slots = recs * cap
    r = lax.axis_index("rec")
    c = lax.axis_index("ctx")
    z = c // parts
    part = c % parts
    factor = 1.0 / math.sqrt(HEAD_DIM)

    def head_cols(rec, group):
        return pl.ds(pl.multiple_of((rec * groups + group) * HEAD_DIM, HEAD_DIM), HEAD_DIM)

    others = [(dr, dz) for dz in range(groups) for dr in range(recs) if dr or dz]

    def partner(dr, dz):
        return (lax.rem(r + dr, recs), lax.rem(z + dz, groups))

    def sibling(dp):
        return lax.rem(part + dp, parts)

    ints = [
        pltpu.make_async_copy(surv_ref, surv, int_sem.at[0]),
        pltpu.make_async_copy(counts_ref, live_counts, int_sem.at[1]),
    ]
    for copy in ints:
        copy.start()

    barrier = pltpu.get_barrier_semaphore()
    for dr, dz in others:
        pr, pz = partner(dr, dz)
        pl.semaphore_signal(barrier, inc=1, device_id=(pr, pz * parts + part), device_id_type=MESH)
    for dp in range(1, parts):
        pl.semaphore_signal(
            barrier, inc=1, device_id=(r, z * parts + sibling(dp)), device_id_type=MESH
        )

    mine = []
    rows_r = pl.ds(pl.multiple_of(r * cap, cap), cap)
    for i, ref in enumerate((q_ref, g_ref)):
        mine.append(pltpu.make_async_copy(
            ref.at[0, :, head_cols(r, z)], qg.at[z, i, rows_r, :], qg_recv.at[z]))
    for i, ref in enumerate((k_ref, v_ref)):
        mine.append(pltpu.make_async_copy(ref.at[:, head_cols(r, z)], kv.at[c, i], kv_recv.at[c]))
    for copy in mine:
        copy.start()

    for copy in ints:
        copy.wait()
    row = jnp.broadcast_to(surv[...], (8, surv.shape[1]))
    lane = lax.broadcasted_iota(jnp.int32, (1, slots), 1)
    here = lane - r * cap
    for zs in range(groups):
        cs = zs * parts + part
        moved = pltpu.roll(row, lax.rem(r * cap - cs * cap + ctxs * cap, ctxs * cap), 1)
        live = (here >= 0) & (here < cap) & (here < live_counts[0, cs])
        pos[r, zs : zs + 1, :] = jnp.where(live, moved[0:1, 0:slots] + cs * tok + 1, 0)

    pl.semaphore_wait(barrier, len(others) + parts - 1)

    sends = []

    def send(src, dst, send_sem, recv_sem, device):
        copy = pltpu.make_async_remote_copy(
            src_ref=src, dst_ref=dst, send_sem=send_sem, recv_sem=recv_sem,
            device_id=device, device_id_type=MESH,
        )
        copy.start()
        sends.append(copy)

    for dz in range(1, groups):
        pz = lax.rem(z + dz, groups)
        for i, ref in enumerate((k_ref, v_ref)):
            send(ref.at[:, head_cols(r, pz)], kv.at[c, i], kv_send.at[dz, i], kv_recv.at[c],
                 (r, pz * parts + part))
    for dr in range(1, recs):
        send(pos.at[r], pos.at[r], pos_send.at[dr], pos_recv.at[r], (lax.rem(r + dr, recs), c))
    for dr, dz in others:
        pr, pz = partner(dr, dz)
        for i, ref in enumerate((q_ref, g_ref)):
            send(ref.at[0, :, head_cols(pr, pz)], qg.at[z, i, rows_r, :],
                 qg_send.at[dz, dr, i], qg_recv.at[z], (pr, pz * parts + part))
    for dp in range(1, parts):
        for i, ref in enumerate((k_ref, v_ref)):
            send(ref.at[:, head_cols(r, z)], kv.at[c, i], fwd_send.at[dp, 0, i], kv_recv.at[c],
                 (r, z * parts + sibling(dp)))

    def arrived(ref, sem):
        pltpu.make_async_copy(ref, ref, sem).wait()

    for dz in range(1, groups):
        cs = lax.rem(z + dz, groups) * parts + part
        arrived(kv.at[cs], kv_recv.at[cs])
        for dp in range(1, parts):
            send(kv.at[cs], kv.at[cs], fwd_send.at[dp, dz, 0], kv_recv.at[cs],
                 (r, z * parts + sibling(dp)))
    arrived(kv.at[c], kv_recv.at[c])
    for dr in range(1, recs):
        rs = lax.rem(r + dr, recs)
        arrived(pos.at[rs], pos_recv.at[rs])
    for dz in range(groups):
        for dp in range(1, parts):
            cs = lax.rem(z + dz, groups) * parts + sibling(dp)
            arrived(kv.at[cs], kv_recv.at[cs])

    place = sum(pos[rs] for rs in range(recs)) - 1

    def finish(zs):
        dkv = acc[zs * parts + part]
        for dp in range(1, parts):
            arrived(peer.at[dp, zs], acc_recv.at[dp, zs])
            dkv += peer[dp, zs]
        dkv_buf[zs, 0] = (dkv[0] * factor).astype(jnp.bfloat16)
        dkv_buf[zs, 1] = dkv[1].astype(jnp.bfloat16)
        cols = pl.ds(pl.multiple_of(z * HEAD_DIM, HEAD_DIM), HEAD_DIM)
        for i, ref in enumerate((dk_ref, dv_ref)):

            @pl.when(z == zs)
            def _():
                pltpu.make_async_copy(dkv_buf.at[zs, i], ref.at[:, cols], dkv_recv.at[i]).start()

            @pl.when(z != zs)
            def _():
                pltpu.make_async_remote_copy(
                    src_ref=dkv_buf.at[zs, i], dst_ref=ref.at[:, cols],
                    send_sem=dkv_send.at[zs, i], recv_sem=dkv_recv.at[i],
                    device_id=(r, zs * parts + part), device_id_type=MESH,
                ).start()

    for zs in reversed(range(groups)):
        blocks = (zs + 1) * parts
        length = blocks * tok
        arrived(qg.at[zs], qg_recv.at[zs])
        q, g = qg[zs, 0], qg[zs, 1]
        keys = kv[0:blocks, 0].reshape(length, HEAD_DIM)
        vals = kv[0:blocks, 1].reshape(length, HEAD_DIM)
        scores = lax.dot_general(keys, q, NT, preferred_element_type=jnp.float32)
        seen = lax.broadcasted_iota(jnp.int32, (length, slots), 0) <= place[zs : zs + 1, :]
        scores = jnp.where(seen, scores * (factor * math.log2(math.e)), NEG_FILL)
        top = jnp.maximum(jnp.max(scores, axis=0, keepdims=True), 0.1 * NEG_FILL)
        raw = jnp.exp2(scores - top)
        total = jnp.sum(raw, axis=0, keepdims=True)
        weights = raw * (1.0 / jnp.maximum(total, 1e-30))
        grads = lax.dot_general(vals, g, NT, preferred_element_type=jnp.float32)
        delta = jnp.sum(weights * grads, axis=0, keepdims=True)
        ds = (weights * (grads - delta)).astype(jnp.bfloat16)
        wb = weights.astype(jnp.bfloat16)
        dq = lax.dot_general(ds, keys, TN, preferred_element_type=jnp.float32)
        dq_buf[zs] = (dq * factor).astype(jnp.bfloat16)
        for rd in range(recs):
            src = dq_buf.at[zs, rd * cap : (rd + 1) * cap, :]
            dst = dq_ref.at[0, :, head_cols(r, z)]
            home = (r == rd) & (z == zs)

            @pl.when(home)
            def _():
                pltpu.make_async_copy(src, dst, dq_recv).start()

            @pl.when(jnp.logical_not(home))
            def _():
                pltpu.make_async_remote_copy(
                    src_ref=src, dst_ref=dst, send_sem=dq_send.at[zs, rd], recv_sem=dq_recv,
                    device_id=(rd, zs * parts + part), device_id_type=MESH,
                ).start()

        dk = lax.dot_general(ds, q, (((1,), (0,)), ((), ())), preferred_element_type=jnp.float32)
        dv = lax.dot_general(wb, g, (((1,), (0,)), ((), ())), preferred_element_type=jnp.float32)
        dk = dk.reshape(blocks, tok, HEAD_DIM)
        dv = dv.reshape(blocks, tok, HEAD_DIM)
        if zs == groups - 1:
            acc[0:blocks, 0] = dk
            acc[0:blocks, 1] = dv
        else:
            acc[0:blocks, 0] += dk
            acc[0:blocks, 1] += dv
        for dp in range(1, parts):
            cd = zs * parts + sibling(dp)
            send(acc.at[cd], peer.at[parts - dp, zs], acc_send.at[dp, zs],
                 acc_recv.at[parts - dp, zs], (r, z * parts + sibling(dp)))
        if zs < groups - 1:
            finish(zs + 1)
    finish(0)


    for copy in sends:
        copy.wait_send()
    for zs in range(groups):
        for rd in range(recs):

            @pl.when(jnp.logical_not((r == rd) & (z == zs)))
            def _():
                arrived(dq_buf.at[zs, rd * cap : (rd + 1) * cap, :], dq_send.at[zs, rd])

        for i in range(2):

            @pl.when(z != zs)
            def _():
                arrived(dkv_buf.at[zs, i], dkv_send.at[zs, i])

    arrived(dq_ref, dq_recv)
    arrived(dk_ref, dkv_recv.at[0])
    arrived(dv_ref, dkv_recv.at[1])


def hand_over(a, b, c, a_out, b_out, c_out, a_here, b_here, c_here, sem):
    trios = ((a, a_here, a_out), (b, b_here, b_out), (c, c_here, c_out))
    into = [pltpu.make_async_copy(src, mid, sem.at[0, i]) for i, (src, mid, _) in enumerate(trios)]
    out = [pltpu.make_async_copy(mid, dst, sem.at[1, i]) for i, (_, mid, dst) in enumerate(trios)]
    for copy in into:
        copy.start()
    for arriving, leaving in zip(into, out):
        arriving.wait()
        leaving.start()
    for copy in out:
        copy.wait()


def body(queries, grad_out, keys, values, surv_index, counts):
    recs = lax.axis_size("rec")
    ctxs = lax.axis_size("ctx")
    cap, tok = queries.shape[1], keys.shape[0]
    groups = HEADS // recs
    parts = ctxs // groups
    slots = recs * cap
    dma = pltpu.SemaphoreType.DMA
    anywhere = pl.BlockSpec(memory_space=pltpu.HBM)
    results = pl.pallas_call(
        functools.partial(kernel, recs, ctxs),
        out_shape=(
            jax.ShapeDtypeStruct(queries.shape, jnp.bfloat16),
            jax.ShapeDtypeStruct((tok, groups * HEAD_DIM), jnp.bfloat16),
            jax.ShapeDtypeStruct((tok, groups * HEAD_DIM), jnp.bfloat16),
        ),
        in_specs=[anywhere] * 6,
        out_specs=(anywhere,) * 3,
        scratch_shapes=[
            pltpu.VMEM(surv_index.shape, jnp.int32),
            pltpu.SMEM(counts.shape, jnp.int32),
            pltpu.VMEM((recs, 8, slots), jnp.int32),
            pltpu.VMEM((groups, 2, slots, HEAD_DIM), jnp.bfloat16),
            pltpu.VMEM((ctxs, 2, tok, HEAD_DIM), jnp.bfloat16),
            pltpu.VMEM((ctxs, 2, tok, HEAD_DIM), jnp.float32),
            pltpu.VMEM((parts, groups, 2, tok, HEAD_DIM), jnp.float32),
            pltpu.VMEM((groups, slots, HEAD_DIM), jnp.bfloat16),
            pltpu.VMEM((groups, 2, tok, HEAD_DIM), jnp.bfloat16),
            dma((2,)), dma((recs,)), dma((recs,)),
            dma((groups, recs, 2)), dma((groups,)),
            dma((groups, 2)), dma((ctxs,)),
            dma((parts, groups, 2)),
            dma((parts, groups)), dma((parts, groups)),
            dma((groups, recs)), dma,
            dma((groups, 2)), dma((2,)),
        ],
        compiler_params=pltpu.CompilerParams(
            collective_id=0, has_side_effects=True, vmem_limit_bytes=64 * 2**20
        ),
        cost_estimate=pl.CostEstimate(
            flops=10 * groups * slots * ctxs * tok * HEAD_DIM,
            bytes_accessed=4 * ctxs * tok * HEAD_DIM * 2,
            transcendentals=groups * slots * ctxs * tok,
        ),
    )(queries, grad_out, keys, values, surv_index, counts)
    return pl.pallas_call(
        hand_over,
        out_shape=tuple(jax.ShapeDtypeStruct(a.shape, a.dtype) for a in results),
        in_specs=[anywhere] * 3,
        out_specs=(anywhere,) * 3,
        scratch_shapes=[pltpu.VMEM(a.shape, a.dtype) for a in results] + [dma((2, 3))],
        compiler_params=pltpu.CompilerParams(vmem_limit_bytes=64 * 2**20),
    )(*results)


def solution(mesh):
    in_specs = (
        P("rec", "ctx", None),
        P("rec", "ctx", None),
        P("ctx", None),
        P("ctx", None),
        P("rec", None),
        P("rec", None),
    )
    out_specs = (P("rec", "ctx", None), P("ctx", "rec"), P("ctx", "rec"))
    return jax.shard_map(body, mesh=mesh, in_specs=in_specs, out_specs=out_specs, check_vma=False)
```

```python
import functools
import math

import jax
import jax.numpy as jnp
from jax import lax
from jax.experimental import pallas as pl
from jax.experimental.pallas import tpu as pltpu
from jax.sharding import PartitionSpec as P

HEADS = 16
HEAD_DIM = 128
NEG_FILL = -1e30
MESH = pl.DeviceIdType.MESH
NT = (((1,), (1,)), ((), ()))
TN = (((0,), (0,)), ((), ()))


def kernel(
    recs, ctxs, q_ref, g_ref, k_ref, v_ref, surv_ref, counts_ref,
    dq_ref, dk_ref, dv_ref,
    surv, live_counts, pos, qg, kv, ds_buf, w_buf, acc, peer, dq_buf, dkv_buf,
    int_sem, pos_send, pos_recv, qg_send, qg_recv, kv_send, kv_recv, fwd_send,
    acc_send, acc_recv, dq_send, dq_recv, dkv_send, dkv_recv,
):
    groups = HEADS // recs
    parts = ctxs // groups
    cap = q_ref.shape[1]
    tok = k_ref.shape[0]
    slots = recs * cap
    r = lax.axis_index("rec")
    c = lax.axis_index("ctx")
    z = c // parts
    part = c % parts
    factor = 1.0 / math.sqrt(HEAD_DIM)

    def head_cols(rec, group):
        return pl.ds(pl.multiple_of((rec * groups + group) * HEAD_DIM, HEAD_DIM), HEAD_DIM)

    others = [(dr, dz) for dz in range(groups) for dr in range(recs) if dr or dz]

    def partner(dr, dz):
        return (lax.rem(r + dr, recs), lax.rem(z + dz, groups))

    def sibling(dp):
        return lax.rem(part + dp, parts)

    ints = [
        pltpu.make_async_copy(surv_ref, surv, int_sem.at[0]),
        pltpu.make_async_copy(counts_ref, live_counts, int_sem.at[1]),
    ]
    for copy in ints:
        copy.start()

    barrier = pltpu.get_barrier_semaphore()
    for dr, dz in others:
        pr, pz = partner(dr, dz)
        pl.semaphore_signal(barrier, inc=1, device_id=(pr, pz * parts + part), device_id_type=MESH)
    for dp in range(1, parts):
        pl.semaphore_signal(
            barrier, inc=1, device_id=(r, z * parts + sibling(dp)), device_id_type=MESH
        )

    mine = []
    rows_r = pl.ds(pl.multiple_of(r * cap, cap), cap)
    for i, ref in enumerate((q_ref, g_ref)):
        mine.append(pltpu.make_async_copy(
            ref.at[0, :, head_cols(r, z)], qg.at[z, i, rows_r, :], qg_recv.at[z]))
    for i, ref in enumerate((k_ref, v_ref)):
        mine.append(pltpu.make_async_copy(ref.at[:, head_cols(r, z)], kv.at[c, i], kv_recv.at[c]))
    for copy in mine:
        copy.start()

    for copy in ints:
        copy.wait()
    row = jnp.broadcast_to(surv[...], (8, surv.shape[1]))
    lane = lax.broadcasted_iota(jnp.int32, (1, slots), 1)
    here = lane - r * cap
    for zs in range(groups):
        cs = zs * parts + part
        moved = pltpu.roll(row, lax.rem(r * cap - cs * cap + ctxs * cap, ctxs * cap), 1)
        live = (here >= 0) & (here < cap) & (here < live_counts[0, cs])
        pos[r, zs : zs + 1, :] = jnp.where(live, moved[0:1, 0:slots] + cs * tok + 1, 0)

    pl.semaphore_wait(barrier, len(others) + parts - 1)

    sends = []

    def send(src, dst, send_sem, recv_sem, device):
        copy = pltpu.make_async_remote_copy(
            src_ref=src, dst_ref=dst, send_sem=send_sem, recv_sem=recv_sem,
            device_id=device, device_id_type=MESH,
        )
        copy.start()
        sends.append(copy)

    for dz in range(1, groups):
        pz = lax.rem(z + dz, groups)
        for i, ref in enumerate((k_ref, v_ref)):
            send(ref.at[:, head_cols(r, pz)], kv.at[c, i], kv_send.at[dz, i], kv_recv.at[c],
                 (r, pz * parts + part))
    for dr in range(1, recs):
        send(pos.at[r], pos.at[r], pos_send.at[dr], pos_recv.at[r], (lax.rem(r + dr, recs), c))
    for dr, dz in others:
        pr, pz = partner(dr, dz)
        for i, ref in enumerate((q_ref, g_ref)):
            send(ref.at[0, :, head_cols(pr, pz)], qg.at[z, i, rows_r, :],
                 qg_send.at[dz, dr, i], qg_recv.at[z], (pr, pz * parts + part))
    for dp in range(1, parts):
        for i, ref in enumerate((k_ref, v_ref)):
            send(ref.at[:, head_cols(r, z)], kv.at[c, i], fwd_send.at[dp, 0, i], kv_recv.at[c],
                 (r, z * parts + sibling(dp)))

    def arrived(ref, sem):
        pltpu.make_async_copy(ref, ref, sem).wait()

    for dz in range(1, groups):
        cs = lax.rem(z + dz, groups) * parts + part
        arrived(kv.at[cs], kv_recv.at[cs])
        for dp in range(1, parts):
            send(kv.at[cs], kv.at[cs], fwd_send.at[dp, dz, 0], kv_recv.at[cs],
                 (r, z * parts + sibling(dp)))
    arrived(kv.at[c], kv_recv.at[c])
    for dr in range(1, recs):
        rs = lax.rem(r + dr, recs)
        arrived(pos.at[rs], pos_recv.at[rs])
    for dz in range(groups):
        for dp in range(1, parts):
            cs = lax.rem(z + dz, groups) * parts + sibling(dp)
            arrived(kv.at[cs], kv_recv.at[cs])

    place = sum(pos[rs] for rs in range(recs)) - 1

    def finish(zs):
        dkv = acc[zs * parts + part]
        for dp in range(1, parts):
            arrived(peer.at[dp, zs], acc_recv.at[dp, zs])
            dkv += peer[dp, zs]
        dkv_buf[zs, 0] = (dkv[0] * factor).astype(jnp.bfloat16)
        dkv_buf[zs, 1] = dkv[1].astype(jnp.bfloat16)
        cols = pl.ds(pl.multiple_of(z * HEAD_DIM, HEAD_DIM), HEAD_DIM)
        for i, ref in enumerate((dk_ref, dv_ref)):

            @pl.when(z == zs)
            def _():
                pltpu.make_async_copy(dkv_buf.at[zs, i], ref.at[:, cols], dkv_recv.at[i]).start()

            @pl.when(z != zs)
            def _():
                pltpu.make_async_remote_copy(
                    src_ref=dkv_buf.at[zs, i], dst_ref=ref.at[:, cols],
                    send_sem=dkv_send.at[zs, i], recv_sem=dkv_recv.at[i],
                    device_id=(r, zs * parts + part), device_id_type=MESH,
                ).start()

    for zs in range(groups):
        blocks = (zs + 1) * parts
        length = blocks * tok
        before = zs * parts * tok
        arrived(qg.at[zs], qg_recv.at[zs])
        q, g = qg[zs, 0], qg[zs, 1]
        keys = kv[0:blocks, 0].reshape(length, HEAD_DIM)
        vals = kv[0:blocks, 1].reshape(length, HEAD_DIM)
        scores = lax.dot_general(keys, q, NT, preferred_element_type=jnp.float32)
        scores = scores * (factor * math.log2(math.e))
        position = place[zs : zs + 1, :]
        seen = lax.broadcasted_iota(jnp.int32, (length - before, slots), 0) + before <= position
        last = jnp.where(seen, scores[before:], NEG_FILL)
        scores = jnp.concatenate([scores[:before], last], axis=0) if before else last
        top = jnp.maximum(jnp.max(scores, axis=0, keepdims=True), 0.1 * NEG_FILL)
        raw = jnp.exp2(scores - top)
        total = jnp.sum(raw, axis=0, keepdims=True)
        weights = raw * jnp.where(position >= 0, 1.0 / jnp.maximum(total, 1e-30), 0.0)
        grads = lax.dot_general(vals, g, NT, preferred_element_type=jnp.float32)
        delta = jnp.sum(weights * grads, axis=0, keepdims=True)
        ds = (weights * (grads - delta)).astype(jnp.bfloat16)
        lanes = slice(zs * slots, (zs + 1) * slots)
        ds_buf[0:length, lanes] = ds
        w_buf[0:length, lanes] = weights.astype(jnp.bfloat16)
        dq = lax.dot_general(ds, keys, TN, preferred_element_type=jnp.float32)
        dq_buf[zs] = (dq * factor).astype(jnp.bfloat16)
        for rd in range(recs):
            src = dq_buf.at[zs, rd * cap : (rd + 1) * cap, :]
            dst = dq_ref.at[0, :, head_cols(r, z)]
            home = (r == rd) & (z == zs)

            @pl.when(home)
            def _():
                pltpu.make_async_copy(src, dst, dq_recv).start()

            @pl.when(jnp.logical_not(home))
            def _():
                pltpu.make_async_remote_copy(
                    src_ref=src, dst_ref=dst, send_sem=dq_send.at[zs, rd], recv_sem=dq_recv,
                    device_id=(rd, zs * parts + part), device_id_type=MESH,
                ).start()

    order = sorted(range(groups), key=lambda zs: (min(zs, groups - 1 - zs), -zs))
    for step, zs in enumerate(order):
        rows = slice(zs * parts * tok, (zs + 1) * parts * tok)
        lanes = slice(zs * slots, groups * slots)
        for i, buf in enumerate((ds_buf, w_buf)):
            right = qg[zs:, i].reshape((groups - zs) * slots, HEAD_DIM)
            term = jnp.dot(buf[rows, lanes], right, preferred_element_type=jnp.float32)
            acc[zs * parts : (zs + 1) * parts, i] = term.reshape(parts, tok, HEAD_DIM)
        for dp in range(1, parts):
            cd = zs * parts + sibling(dp)
            send(acc.at[cd], peer.at[parts - dp, zs], acc_send.at[dp, zs],
                 acc_recv.at[parts - dp, zs], (r, z * parts + sibling(dp)))
        if step:
            finish(order[step - 1])
    finish(order[-1])

    for copy in sends:
        copy.wait_send()
    for zs in range(groups):
        for rd in range(recs):

            @pl.when(jnp.logical_not((r == rd) & (z == zs)))
            def _():
                arrived(dq_buf.at[zs, rd * cap : (rd + 1) * cap, :], dq_send.at[zs, rd])

        for i in range(2):

            @pl.when(z != zs)
            def _():
                arrived(dkv_buf.at[zs, i], dkv_send.at[zs, i])

    arrived(dq_ref, dq_recv)
    arrived(dk_ref, dkv_recv.at[0])
    arrived(dv_ref, dkv_recv.at[1])


def hand_over(a, b, c, a_out, b_out, c_out, a_here, b_here, c_here, sem):
    trios = ((a, a_here, a_out), (b, b_here, b_out), (c, c_here, c_out))
    into = [pltpu.make_async_copy(src, mid, sem.at[0, i]) for i, (src, mid, _) in enumerate(trios)]
    out = [pltpu.make_async_copy(mid, dst, sem.at[1, i]) for i, (_, mid, dst) in enumerate(trios)]
    for copy in into:
        copy.start()
    for arriving, leaving in zip(into, out):
        arriving.wait()
        leaving.start()
    for copy in out:
        copy.wait()


def body(queries, grad_out, keys, values, surv_index, counts):
    recs = lax.axis_size("rec")
    ctxs = lax.axis_size("ctx")
    cap, tok = queries.shape[1], keys.shape[0]
    groups = HEADS // recs
    parts = ctxs // groups
    slots = recs * cap
    dma = pltpu.SemaphoreType.DMA
    anywhere = pl.BlockSpec(memory_space=pltpu.HBM)
    results = pl.pallas_call(
        functools.partial(kernel, recs, ctxs),
        out_shape=(
            jax.ShapeDtypeStruct(queries.shape, jnp.bfloat16),
            jax.ShapeDtypeStruct((tok, groups * HEAD_DIM), jnp.bfloat16),
            jax.ShapeDtypeStruct((tok, groups * HEAD_DIM), jnp.bfloat16),
        ),
        in_specs=[anywhere] * 6,
        out_specs=(anywhere,) * 3,
        scratch_shapes=[
            pltpu.VMEM(surv_index.shape, jnp.int32),
            pltpu.SMEM(counts.shape, jnp.int32),
            pltpu.VMEM((recs, 8, slots), jnp.int32),
            pltpu.VMEM((groups, 2, slots, HEAD_DIM), jnp.bfloat16),
            pltpu.VMEM((ctxs, 2, tok, HEAD_DIM), jnp.bfloat16),
            pltpu.VMEM((ctxs * tok, groups * slots), jnp.bfloat16),
            pltpu.VMEM((ctxs * tok, groups * slots), jnp.bfloat16),
            pltpu.VMEM((ctxs, 2, tok, HEAD_DIM), jnp.float32),
            pltpu.VMEM((parts, groups, 2, tok, HEAD_DIM), jnp.float32),
            pltpu.VMEM((groups, slots, HEAD_DIM), jnp.bfloat16),
            pltpu.VMEM((groups, 2, tok, HEAD_DIM), jnp.bfloat16),
            dma((2,)), dma((recs,)), dma((recs,)),
            dma((groups, recs, 2)), dma((groups,)),
            dma((groups, 2)), dma((ctxs,)),
            dma((parts, groups, 2)),
            dma((parts, groups)), dma((parts, groups)),
            dma((groups, recs)), dma,
            dma((groups, 2)), dma((2,)),
        ],
        compiler_params=pltpu.CompilerParams(
            collective_id=0, has_side_effects=True, vmem_limit_bytes=64 * 2**20
        ),
        cost_estimate=pl.CostEstimate(
            flops=10 * groups * slots * ctxs * tok * HEAD_DIM,
            bytes_accessed=4 * ctxs * tok * HEAD_DIM * 2,
            transcendentals=groups * slots * ctxs * tok,
        ),
    )(queries, grad_out, keys, values, surv_index, counts)
    return pl.pallas_call(
        hand_over,
        out_shape=tuple(jax.ShapeDtypeStruct(a.shape, a.dtype) for a in results),
        in_specs=[anywhere] * 3,
        out_specs=(anywhere,) * 3,
        scratch_shapes=[pltpu.VMEM(a.shape, a.dtype) for a in results] + [dma((2, 3))],
        compiler_params=pltpu.CompilerParams(vmem_limit_bytes=64 * 2**20),
    )(*results)


def solution(mesh):
    in_specs = (
        P("rec", "ctx", None),
        P("rec", "ctx", None),
        P("ctx", None),
        P("ctx", None),
        P("rec", None),
        P("rec", None),
    )
    out_specs = (P("rec", "ctx", None), P("ctx", "rec"), P("ctx", "rec"))
    return jax.shard_map(body, mesh=mesh, in_specs=in_specs, out_specs=out_specs, check_vma=False)
```

```python
import functools
import math

import jax
import jax.numpy as jnp
from jax import lax
from jax.experimental import pallas as pl
from jax.experimental.pallas import tpu as pltpu
from jax.sharding import PartitionSpec as P

HEADS = 16
HEAD_DIM = 128
NEG_FILL = -1e30
MESH = pl.DeviceIdType.MESH
NT = (((1,), (1,)), ((), ()))
TN = (((0,), (0,)), ((), ()))


def kernel(
    recs, ctxs, q_ref, g_ref, k_ref, v_ref, surv_ref, counts_ref,
    dq_ref, dk_ref, dv_ref,
    surv, live_counts, pos, qg, kv, ds_buf, w_buf, acc, peer, dq_buf, dkv_buf,
    int_sem, pos_send, pos_recv, qg_send, qg_recv, kv_send, kv_recv, fwd_send,
    acc_send, acc_recv, dq_send, dq_recv, dkv_send, dkv_recv,
):
    groups = HEADS // recs
    parts = ctxs // groups
    cap = q_ref.shape[1]
    tok = k_ref.shape[0]
    slots = recs * cap
    r = lax.axis_index("rec")
    c = lax.axis_index("ctx")
    z = c // parts
    part = c % parts
    factor = 1.0 / math.sqrt(HEAD_DIM)

    def head_cols(rec, group):
        return pl.ds(pl.multiple_of((rec * groups + group) * HEAD_DIM, HEAD_DIM), HEAD_DIM)

    others = [(dr, dz) for dz in range(groups) for dr in range(recs) if dr or dz]

    def flip(index, bits):
        bit = 1
        while bit <= bits:
            if bits & bit:
                index = index + bit * (1 - 2 * (index // bit % 2))
            bit *= 2
        return index

    def partner(dr, dz):
        return (flip(r, dr), flip(z, dz))

    def sibling(dp):
        return lax.rem(part + dp, parts)

    ints = [
        pltpu.make_async_copy(surv_ref, surv, int_sem.at[0]),
        pltpu.make_async_copy(counts_ref, live_counts, int_sem.at[1]),
    ]
    for copy in ints:
        copy.start()

    barrier = pltpu.get_barrier_semaphore()
    for dr, dz in others:
        pr, pz = partner(dr, dz)
        pl.semaphore_signal(barrier, inc=1, device_id=(pr, pz * parts + part), device_id_type=MESH)
    for dp in range(1, parts):
        pl.semaphore_signal(
            barrier, inc=1, device_id=(r, z * parts + sibling(dp)), device_id_type=MESH
        )

    mine = []
    rows_r = pl.ds(pl.multiple_of(r * cap, cap), cap)
    for i, ref in enumerate((q_ref, g_ref)):
        mine.append(pltpu.make_async_copy(
            ref.at[0, :, head_cols(r, z)], qg.at[z, i, rows_r, :], qg_recv.at[z]))
    for i, ref in enumerate((k_ref, v_ref)):
        mine.append(pltpu.make_async_copy(ref.at[:, head_cols(r, z)], kv.at[c, i], kv_recv.at[c]))
    for copy in mine:
        copy.start()

    for copy in ints:
        copy.wait()
    row = jnp.broadcast_to(surv[...], (8, surv.shape[1]))
    lane = lax.broadcasted_iota(jnp.int32, (1, slots), 1)
    here = lane - r * cap
    for zs in range(groups):
        cs = zs * parts + part
        moved = pltpu.roll(row, lax.rem(r * cap - cs * cap + ctxs * cap, ctxs * cap), 1)
        live = (here >= 0) & (here < cap) & (here < live_counts[0, cs])
        pos[r, zs : zs + 1, :] = jnp.where(live, moved[0:1, 0:slots] + cs * tok + 1, 0)

    pl.semaphore_wait(barrier, len(others) + parts - 1)

    sends = []

    def send(src, dst, send_sem, recv_sem, device):
        copy = pltpu.make_async_remote_copy(
            src_ref=src, dst_ref=dst, send_sem=send_sem, recv_sem=recv_sem,
            device_id=device, device_id_type=MESH,
        )
        copy.start()
        sends.append(copy)

    def send_keys(dz):
        pz = flip(z, dz)
        for i, ref in enumerate((k_ref, v_ref)):
            send(ref.at[:, head_cols(r, pz)], kv.at[c, i], kv_send.at[dz, i], kv_recv.at[c],
                 (r, pz * parts + part))

    def send_queries(dz):
        for dr in range(recs):
            if dr or dz:
                pr, pz = partner(dr, dz)
                for i, ref in enumerate((q_ref, g_ref)):
                    send(ref.at[0, :, head_cols(pr, pz)], qg.at[z, i, rows_r, :],
                         qg_send.at[dz, dr, i], qg_recv.at[z], (pr, pz * parts + part))

    far = [dz for dz in reversed(range(1, groups)) if 2 * dz >= groups]
    near = [dz for dz in reversed(range(1, groups)) if 2 * dz < groups]
    for some in (far, near):
        for dz in some:
            send_keys(dz)
        for dz in some:
            send_queries(dz)
    send_queries(0)
    for dr in range(1, recs):
        send(pos.at[r], pos.at[r], pos_send.at[dr], pos_recv.at[r], (flip(r, dr), c))
    for dp in range(1, parts):
        for i, ref in enumerate((k_ref, v_ref)):
            send(ref.at[:, head_cols(r, z)], kv.at[c, i], fwd_send.at[dp, 0, i], kv_recv.at[c],
                 (r, z * parts + sibling(dp)))

    def arrived(ref, sem):
        pltpu.make_async_copy(ref, ref, sem).wait()

    for dz in far + near:
        cs = flip(z, dz) * parts + part
        arrived(kv.at[cs], kv_recv.at[cs])
        for dp in range(1, parts):
            send(kv.at[cs], kv.at[cs], fwd_send.at[dp, dz, 0], kv_recv.at[cs],
                 (r, z * parts + sibling(dp)))
    arrived(kv.at[c], kv_recv.at[c])
    for dr in range(1, recs):
        rs = flip(r, dr)
        arrived(pos.at[rs], pos_recv.at[rs])

    place = sum(pos[rs] for rs in range(recs)) - 1

    def finish(zs):
        dkv = acc[zs * parts + part]
        for dp in range(1, parts):
            arrived(peer.at[dp, zs], acc_recv.at[dp, zs])
            dkv += peer[dp, zs]
        dkv_buf[zs, 0] = (dkv[0] * factor).astype(jnp.bfloat16)
        dkv_buf[zs, 1] = dkv[1].astype(jnp.bfloat16)
        cols = pl.ds(pl.multiple_of(z * HEAD_DIM, HEAD_DIM), HEAD_DIM)
        for i, ref in enumerate((dk_ref, dv_ref)):

            @pl.when(z == zs)
            def _():
                pltpu.make_async_copy(dkv_buf.at[zs, i], ref.at[:, cols], dkv_recv.at[i]).start()

            @pl.when(z != zs)
            def _():
                pltpu.make_async_remote_copy(
                    src_ref=dkv_buf.at[zs, i], dst_ref=ref.at[:, cols],
                    send_sem=dkv_send.at[zs, i], recv_sem=dkv_recv.at[i],
                    device_id=(r, zs * parts + part), device_id_type=MESH,
                ).start()

    for zs in range(groups):
        blocks = (zs + 1) * parts
        length = blocks * tok
        before = zs * parts * tok
        for dp in range(1, parts):
            cs = zs * parts + sibling(dp)
            arrived(kv.at[cs], kv_recv.at[cs])
        arrived(qg.at[zs], qg_recv.at[zs])
        q, g = qg[zs, 0], qg[zs, 1]
        keys = kv[0:blocks, 0].reshape(length, HEAD_DIM)
        vals = kv[0:blocks, 1].reshape(length, HEAD_DIM)
        scores = lax.dot_general(keys, q, NT, preferred_element_type=jnp.float32)
        scores = scores * (factor * math.log2(math.e))
        position = place[zs : zs + 1, :]
        seen = lax.broadcasted_iota(jnp.int32, (length - before, slots), 0) + before <= position
        last = jnp.where(seen, scores[before:], NEG_FILL)
        scores = jnp.concatenate([scores[:before], last], axis=0) if before else last
        top = jnp.maximum(jnp.max(scores, axis=0, keepdims=True), 0.1 * NEG_FILL)
        raw = jnp.exp2(scores - top)
        total = jnp.sum(raw, axis=0, keepdims=True)
        weights = raw * jnp.where(position >= 0, 1.0 / jnp.maximum(total, 1e-30), 0.0)
        grads = lax.dot_general(vals, g, NT, preferred_element_type=jnp.float32)
        delta = jnp.sum(weights * grads, axis=0, keepdims=True)
        ds = (weights * (grads - delta)).astype(jnp.bfloat16)
        lanes = slice(zs * slots, (zs + 1) * slots)
        ds_buf[0:length, lanes] = ds
        w_buf[0:length, lanes] = weights.astype(jnp.bfloat16)
        dq = lax.dot_general(ds, keys, TN, preferred_element_type=jnp.float32)
        dq_buf[zs] = (dq * factor).astype(jnp.bfloat16)
        for rd in range(recs):
            src = dq_buf.at[zs, rd * cap : (rd + 1) * cap, :]
            dst = dq_ref.at[0, :, head_cols(r, z)]
            home = (r == rd) & (z == zs)

            @pl.when(home)
            def _():
                pltpu.make_async_copy(src, dst, dq_recv).start()

            @pl.when(jnp.logical_not(home))
            def _():
                pltpu.make_async_remote_copy(
                    src_ref=src, dst_ref=dst, send_sem=dq_send.at[zs, rd], recv_sem=dq_recv,
                    device_id=(rd, zs * parts + part), device_id_type=MESH,
                ).start()

    order = sorted(range(groups), key=lambda zs: (min(zs, groups - 1 - zs), -zs))
    for step, zs in enumerate(order):
        rows = slice(zs * parts * tok, (zs + 1) * parts * tok)
        lanes = slice(zs * slots, groups * slots)
        for i, buf in enumerate((ds_buf, w_buf)):
            right = qg[zs:, i].reshape((groups - zs) * slots, HEAD_DIM)
            term = jnp.dot(buf[rows, lanes], right, preferred_element_type=jnp.float32)
            acc[zs * parts : (zs + 1) * parts, i] = term.reshape(parts, tok, HEAD_DIM)
        for dp in range(1, parts):
            cd = zs * parts + sibling(dp)
            send(acc.at[cd], peer.at[parts - dp, zs], acc_send.at[dp, zs],
                 acc_recv.at[parts - dp, zs], (r, z * parts + sibling(dp)))
        if step:
            finish(order[step - 1])
    finish(order[-1])

    for copy in sends:
        copy.wait_send()
    for zs in range(groups):
        for rd in range(recs):

            @pl.when(jnp.logical_not((r == rd) & (z == zs)))
            def _():
                arrived(dq_buf.at[zs, rd * cap : (rd + 1) * cap, :], dq_send.at[zs, rd])

        for i in range(2):

            @pl.when(z != zs)
            def _():
                arrived(dkv_buf.at[zs, i], dkv_send.at[zs, i])

    arrived(dq_ref, dq_recv)
    arrived(dk_ref, dkv_recv.at[0])
    arrived(dv_ref, dkv_recv.at[1])


def hand_over(a, b, c, a_out, b_out, c_out, a_here, b_here, c_here, sem):
    trios = ((a, a_here, a_out), (b, b_here, b_out), (c, c_here, c_out))
    into = [pltpu.make_async_copy(src, mid, sem.at[0, i]) for i, (src, mid, _) in enumerate(trios)]
    out = [pltpu.make_async_copy(mid, dst, sem.at[1, i]) for i, (_, mid, dst) in enumerate(trios)]
    for copy in into:
        copy.start()
    for arriving, leaving in zip(into, out):
        arriving.wait()
        leaving.start()
    for copy in out:
        copy.wait()


def body(queries, grad_out, keys, values, surv_index, counts):
    recs = lax.axis_size("rec")
    ctxs = lax.axis_size("ctx")
    cap, tok = queries.shape[1], keys.shape[0]
    groups = HEADS // recs
    parts = ctxs // groups
    slots = recs * cap
    dma = pltpu.SemaphoreType.DMA
    anywhere = pl.BlockSpec(memory_space=pltpu.HBM)
    results = pl.pallas_call(
        functools.partial(kernel, recs, ctxs),
        out_shape=(
            jax.ShapeDtypeStruct(queries.shape, jnp.bfloat16),
            jax.ShapeDtypeStruct((tok, groups * HEAD_DIM), jnp.bfloat16),
            jax.ShapeDtypeStruct((tok, groups * HEAD_DIM), jnp.bfloat16),
        ),
        in_specs=[anywhere] * 6,
        out_specs=(anywhere,) * 3,
        scratch_shapes=[
            pltpu.VMEM(surv_index.shape, jnp.int32),
            pltpu.SMEM(counts.shape, jnp.int32),
            pltpu.VMEM((recs, 8, slots), jnp.int32),
            pltpu.VMEM((groups, 2, slots, HEAD_DIM), jnp.bfloat16),
            pltpu.VMEM((ctxs, 2, tok, HEAD_DIM), jnp.bfloat16),
            pltpu.VMEM((ctxs * tok, groups * slots), jnp.bfloat16),
            pltpu.VMEM((ctxs * tok, groups * slots), jnp.bfloat16),
            pltpu.VMEM((ctxs, 2, tok, HEAD_DIM), jnp.float32),
            pltpu.VMEM((parts, groups, 2, tok, HEAD_DIM), jnp.float32),
            pltpu.VMEM((groups, slots, HEAD_DIM), jnp.bfloat16),
            pltpu.VMEM((groups, 2, tok, HEAD_DIM), jnp.bfloat16),
            dma((2,)), dma((recs,)), dma((recs,)),
            dma((groups, recs, 2)), dma((groups,)),
            dma((groups, 2)), dma((ctxs,)),
            dma((parts, groups, 2)),
            dma((parts, groups)), dma((parts, groups)),
            dma((groups, recs)), dma,
            dma((groups, 2)), dma((2,)),
        ],
        compiler_params=pltpu.CompilerParams(
            collective_id=0, has_side_effects=True, vmem_limit_bytes=64 * 2**20
        ),
        cost_estimate=pl.CostEstimate(
            flops=10 * groups * slots * ctxs * tok * HEAD_DIM,
            bytes_accessed=4 * ctxs * tok * HEAD_DIM * 2,
            transcendentals=groups * slots * ctxs * tok,
        ),
    )(queries, grad_out, keys, values, surv_index, counts)
    return pl.pallas_call(
        hand_over,
        out_shape=tuple(jax.ShapeDtypeStruct(a.shape, a.dtype) for a in results),
        in_specs=[anywhere] * 3,
        out_specs=(anywhere,) * 3,
        scratch_shapes=[pltpu.VMEM(a.shape, a.dtype) for a in results] + [dma((2, 3))],
        compiler_params=pltpu.CompilerParams(vmem_limit_bytes=64 * 2**20),
    )(*results)


def solution(mesh):
    in_specs = (
        P("rec", "ctx", None),
        P("rec", "ctx", None),
        P("ctx", None),
        P("ctx", None),
        P("rec", None),
        P("rec", None),
    )
    out_specs = (P("rec", "ctx", None), P("ctx", "rec"), P("ctx", "rec"))
    return jax.shard_map(body, mesh=mesh, in_specs=in_specs, out_specs=out_specs, check_vma=False)
```

```python
import functools
import math

import jax
import jax.numpy as jnp
from jax import lax
from jax.experimental import pallas as pl
from jax.experimental.pallas import tpu as pltpu
from jax.sharding import PartitionSpec as P

HEADS = 16
HEAD_DIM = 128
NEG_FILL = -1e30
MESH = pl.DeviceIdType.MESH
NT = (((1,), (1,)), ((), ()))
TN = (((0,), (0,)), ((), ()))


def kernel(
    recs, ctxs, q_ref, g_ref, k_ref, v_ref, surv_ref, counts_ref,
    dq_ref, dk_ref, dv_ref,
    surv, live_counts, pos, qg, kv, ds_buf, w_buf, acc, peer, dq_buf, dkv_buf,
    int_sem, pos_send, pos_recv, qg_send, qg_recv, kv_send, kv_recv, fwd_send,
    acc_send, acc_recv, dq_send, dq_recv, dkv_send, dkv_recv,
):
    groups = HEADS // recs
    parts = ctxs // groups
    cap = q_ref.shape[1]
    tok = k_ref.shape[0]
    slots = recs * cap
    r = lax.axis_index("rec")
    c = lax.axis_index("ctx")
    z = c // parts
    part = c % parts
    factor = 1.0 / math.sqrt(HEAD_DIM)

    def head_cols(rec, group):
        return pl.ds(pl.multiple_of((rec * groups + group) * HEAD_DIM, HEAD_DIM), HEAD_DIM)

    def loop(low, high, step):
        lax.fori_loop(low, high, lambda i, carry: (step(i), carry)[1], 0)

    def turn_rec(dr):
        return lax.rem(r + dr, recs)

    def turn_group(dz):
        return lax.rem(z + dz, groups)

    def sibling(dp):
        return lax.rem(part + dp, parts)

    ints = [
        pltpu.make_async_copy(surv_ref, surv, int_sem.at[0]),
        pltpu.make_async_copy(counts_ref, live_counts, int_sem.at[1]),
    ]
    for copy in ints:
        copy.start()

    barrier = pltpu.get_barrier_semaphore()
    def greet(i):
        pl.semaphore_signal(
            barrier, inc=1,
            device_id=(turn_rec(lax.rem(i, recs)), turn_group(i // recs) * parts + part),
            device_id_type=MESH,
        )

    loop(1, recs * groups, greet)
    for dp in range(1, parts):
        pl.semaphore_signal(
            barrier, inc=1, device_id=(r, z * parts + sibling(dp)), device_id_type=MESH
        )

    mine = []
    rows_r = pl.ds(pl.multiple_of(r * cap, cap), cap)
    for i, ref in enumerate((q_ref, g_ref)):
        mine.append(pltpu.make_async_copy(
            ref.at[0, :, head_cols(r, z)], qg.at[z, i, rows_r, :], qg_recv.at[z]))
    for i, ref in enumerate((k_ref, v_ref)):
        mine.append(pltpu.make_async_copy(ref.at[:, head_cols(r, z)], kv.at[c, i], kv_recv.at[c]))
    for copy in mine:
        copy.start()

    for copy in ints:
        copy.wait()
    row = jnp.broadcast_to(surv[...], (8, surv.shape[1]))
    lane = lax.broadcasted_iota(jnp.int32, (1, slots), 1)
    here = lane - r * cap
    for zs in range(groups):
        cs = zs * parts + part
        moved = pltpu.roll(row, lax.rem(r * cap - cs * cap + ctxs * cap, ctxs * cap), 1)
        live = (here >= 0) & (here < cap) & (here < live_counts[0, cs])
        pos[r, zs : zs + 1, :] = jnp.where(live, moved[0:1, 0:slots] + cs * tok + 1, 0)

    pl.semaphore_wait(barrier, recs * groups + parts - 2)

    def remote(src, dst, send_sem, recv_sem, device):
        return pltpu.make_async_remote_copy(
            src_ref=src, dst_ref=dst, send_sem=send_sem, recv_sem=recv_sem,
            device_id=device, device_id_type=MESH,
        )

    def arrived(ref, sem):
        pltpu.make_async_copy(ref, ref, sem).wait()

    def key_copies(dz):
        pz = turn_group(dz)
        return [
            remote(ref.at[:, head_cols(r, pz)], kv.at[c, i], kv_send.at[dz, i], kv_recv.at[c],
                   (r, pz * parts + part))
            for i, ref in enumerate((k_ref, v_ref))
        ]

    def query_copies(n):
        dr, dz = lax.rem(n, recs), n // recs
        pr, pz = turn_rec(dr), turn_group(dz)
        return [
            remote(ref.at[0, :, head_cols(pr, pz)], qg.at[z, i, rows_r, :],
                   qg_send.at[dz, dr, i], qg_recv.at[z], (pr, pz * parts + part))
            for i, ref in enumerate((q_ref, g_ref))
        ]

    def own_key_copies(dp):
        return [
            remote(ref.at[:, head_cols(r, z)], kv.at[c, i], fwd_send.at[dp, 0, i], kv_recv.at[c],
                   (r, z * parts + sibling(dp)))
            for i, ref in enumerate((k_ref, v_ref))
        ]

    def handed_on(dz, dp):
        cs = turn_group(dz) * parts + part
        return remote(kv.at[cs], kv.at[cs], fwd_send.at[dp, dz, 0], kv_recv.at[cs],
                      (r, z * parts + sibling(dp)))

    def place_copy(dr):
        return remote(pos.at[r], pos.at[r], pos_send.at[dr], pos_recv.at[r], (turn_rec(dr), c))

    def sums_copy(zs, dp):
        return remote(acc.at[zs * parts + sibling(dp)], peer.at[parts - dp, zs],
                      acc_send.at[dp, zs], acc_recv.at[parts - dp, zs],
                      (r, z * parts + sibling(dp)))

    def start(copies):
        for copy in copies:
            copy.start()

    def wait_sent(copies):
        for copy in copies:
            copy.wait_send()

    loop(1, groups, lambda dz: start(key_copies(dz)))
    loop(1, recs, lambda dr: start([place_copy(dr)]))
    loop(1, recs * groups, lambda n: start(query_copies(n)))
    loop(1, parts, lambda dp: start(own_key_copies(dp)))

    def hand_on(dz):
        cs = turn_group(dz) * parts + part
        arrived(kv.at[cs], kv_recv.at[cs])
        loop(1, parts, lambda dp: start([handed_on(dz, dp)]))

    loop(1, groups, hand_on)
    arrived(kv.at[c], kv_recv.at[c])
    loop(1, recs, lambda dr: arrived(pos.at[turn_rec(dr)], pos_recv.at[turn_rec(dr)]))

    place = sum(pos[rs] for rs in range(recs)) - 1

    def finish(zs):
        dkv = acc[zs * parts + part]
        for dp in range(1, parts):
            arrived(peer.at[dp, zs], acc_recv.at[dp, zs])
            dkv += peer[dp, zs]
        dkv_buf[zs, 0] = (dkv[0] * factor).astype(jnp.bfloat16)
        dkv_buf[zs, 1] = dkv[1].astype(jnp.bfloat16)
        cols = pl.ds(pl.multiple_of(z * HEAD_DIM, HEAD_DIM), HEAD_DIM)
        for i, ref in enumerate((dk_ref, dv_ref)):

            @pl.when(z == zs)
            def _():
                pltpu.make_async_copy(dkv_buf.at[zs, i], ref.at[:, cols], dkv_recv.at[i]).start()

            @pl.when(z != zs)
            def _():
                pltpu.make_async_remote_copy(
                    src_ref=dkv_buf.at[zs, i], dst_ref=ref.at[:, cols],
                    send_sem=dkv_send.at[zs, i], recv_sem=dkv_recv.at[i],
                    device_id=(r, zs * parts + part), device_id_type=MESH,
                ).start()

    for zs in range(groups):
        blocks = (zs + 1) * parts
        length = blocks * tok
        before = zs * parts * tok
        for dp in range(1, parts):
            cs = zs * parts + sibling(dp)
            arrived(kv.at[cs], kv_recv.at[cs])
        arrived(qg.at[zs], qg_recv.at[zs])
        q, g = qg[zs, 0], qg[zs, 1]
        keys = kv[0:blocks, 0].reshape(length, HEAD_DIM)
        vals = kv[0:blocks, 1].reshape(length, HEAD_DIM)
        scores = lax.dot_general(keys, q, NT, preferred_element_type=jnp.float32)
        scores = scores * (factor * math.log2(math.e))
        position = place[zs : zs + 1, :]
        seen = lax.broadcasted_iota(jnp.int32, (length - before, slots), 0) + before <= position
        last = jnp.where(seen, scores[before:], NEG_FILL)
        scores = jnp.concatenate([scores[:before], last], axis=0) if before else last
        top = jnp.maximum(jnp.max(scores, axis=0, keepdims=True), 0.1 * NEG_FILL)
        raw = jnp.exp2(scores - top)
        total = jnp.sum(raw, axis=0, keepdims=True)
        weights = raw * jnp.where(position >= 0, 1.0 / jnp.maximum(total, 1e-30), 0.0)
        grads = lax.dot_general(vals, g, NT, preferred_element_type=jnp.float32)
        delta = jnp.sum(weights * grads, axis=0, keepdims=True)
        ds = (weights * (grads - delta)).astype(jnp.bfloat16)
        lanes = slice(zs * slots, (zs + 1) * slots)
        ds_buf[0:length, lanes] = ds
        w_buf[0:length, lanes] = weights.astype(jnp.bfloat16)
        dq = lax.dot_general(ds, keys, TN, preferred_element_type=jnp.float32)
        dq_buf[zs] = (dq * factor).astype(jnp.bfloat16)

        def send_home(rd):
            src = dq_buf.at[zs, pl.ds(pl.multiple_of(rd * cap, cap), cap), :]
            dst = dq_ref.at[0, :, head_cols(r, z)]
            home = (r == rd) & (z == zs)

            @pl.when(home)
            def _():
                pltpu.make_async_copy(src, dst, dq_recv).start()

            @pl.when(jnp.logical_not(home))
            def _():
                remote(src, dst, dq_send.at[zs, rd], dq_recv, (rd, zs * parts + part)).start()

        loop(0, recs, send_home)

    order = sorted(range(groups), key=lambda zs: (min(zs, groups - 1 - zs), -zs))
    for step, zs in enumerate(order):
        rows = slice(zs * parts * tok, (zs + 1) * parts * tok)
        lanes = slice(zs * slots, groups * slots)
        for i, buf in enumerate((ds_buf, w_buf)):
            right = qg[zs:, i].reshape((groups - zs) * slots, HEAD_DIM)
            term = jnp.dot(buf[rows, lanes], right, preferred_element_type=jnp.float32)
            acc[zs * parts : (zs + 1) * parts, i] = term.reshape(parts, tok, HEAD_DIM)
        loop(1, parts, lambda dp: start([sums_copy(zs, dp)]))
        if step:
            finish(order[step - 1])
    finish(order[-1])

    loop(1, groups, lambda dz: wait_sent(key_copies(dz)))
    loop(1, recs, lambda dr: wait_sent([place_copy(dr)]))
    loop(1, recs * groups, lambda n: wait_sent(query_copies(n)))
    loop(1, parts, lambda dp: wait_sent(own_key_copies(dp)))
    loop(1, groups, lambda dz: loop(1, parts, lambda dp: wait_sent([handed_on(dz, dp)])))
    loop(0, groups, lambda zs: loop(1, parts, lambda dp: wait_sent([sums_copy(zs, dp)])))

    def sent_home(n):
        zs, rd = n // recs, lax.rem(n, recs)

        @pl.when(jnp.logical_not((r == rd) & (z == zs)))
        def _():
            arrived(dq_buf.at[zs, pl.ds(pl.multiple_of(rd * cap, cap), cap), :], dq_send.at[zs, rd])

    def sums_sent(zs):
        @pl.when(z != zs)
        def _():
            for i in range(2):
                arrived(dkv_buf.at[zs, i], dkv_send.at[zs, i])

    loop(0, recs * groups, sent_home)
    loop(0, groups, sums_sent)
    arrived(dq_ref, dq_recv)
    arrived(dk_ref, dkv_recv.at[0])
    arrived(dv_ref, dkv_recv.at[1])


def hand_over(a, b, c, a_out, b_out, c_out, a_here, b_here, c_here, sem):
    trios = ((a, a_here, a_out), (b, b_here, b_out), (c, c_here, c_out))
    into = [pltpu.make_async_copy(src, mid, sem.at[0, i]) for i, (src, mid, _) in enumerate(trios)]
    out = [pltpu.make_async_copy(mid, dst, sem.at[1, i]) for i, (_, mid, dst) in enumerate(trios)]
    for copy in into:
        copy.start()
    for arriving, leaving in zip(into, out):
        arriving.wait()
        leaving.start()
    for copy in out:
        copy.wait()


def body(queries, grad_out, keys, values, surv_index, counts):
    recs = lax.axis_size("rec")
    ctxs = lax.axis_size("ctx")
    cap, tok = queries.shape[1], keys.shape[0]
    groups = HEADS // recs
    parts = ctxs // groups
    slots = recs * cap
    dma = pltpu.SemaphoreType.DMA
    anywhere = pl.BlockSpec(memory_space=pltpu.HBM)
    results = pl.pallas_call(
        functools.partial(kernel, recs, ctxs),
        out_shape=(
            jax.ShapeDtypeStruct(queries.shape, jnp.bfloat16),
            jax.ShapeDtypeStruct((tok, groups * HEAD_DIM), jnp.bfloat16),
            jax.ShapeDtypeStruct((tok, groups * HEAD_DIM), jnp.bfloat16),
        ),
        in_specs=[anywhere] * 6,
        out_specs=(anywhere,) * 3,
        scratch_shapes=[
            pltpu.VMEM(surv_index.shape, jnp.int32),
            pltpu.SMEM(counts.shape, jnp.int32),
            pltpu.VMEM((recs, 8, slots), jnp.int32),
            pltpu.VMEM((groups, 2, slots, HEAD_DIM), jnp.bfloat16),
            pltpu.VMEM((ctxs, 2, tok, HEAD_DIM), jnp.bfloat16),
            pltpu.VMEM((ctxs * tok, groups * slots), jnp.bfloat16),
            pltpu.VMEM((ctxs * tok, groups * slots), jnp.bfloat16),
            pltpu.VMEM((ctxs, 2, tok, HEAD_DIM), jnp.float32),
            pltpu.VMEM((parts, groups, 2, tok, HEAD_DIM), jnp.float32),
            pltpu.VMEM((groups, slots, HEAD_DIM), jnp.bfloat16),
            pltpu.VMEM((groups, 2, tok, HEAD_DIM), jnp.bfloat16),
            dma((2,)), dma((recs,)), dma((recs,)),
            dma((groups, recs, 2)), dma((groups,)),
            dma((groups, 2)), dma((ctxs,)),
            dma((parts, groups, 2)),
            dma((parts, groups)), dma((parts, groups)),
            dma((groups, recs)), dma,
            dma((groups, 2)), dma((2,)),
        ],
        compiler_params=pltpu.CompilerParams(
            collective_id=0, has_side_effects=True, vmem_limit_bytes=64 * 2**20
        ),
        cost_estimate=pl.CostEstimate(
            flops=10 * groups * slots * ctxs * tok * HEAD_DIM,
            bytes_accessed=4 * ctxs * tok * HEAD_DIM * 2,
            transcendentals=groups * slots * ctxs * tok,
        ),
    )(queries, grad_out, keys, values, surv_index, counts)
    return pl.pallas_call(
        hand_over,
        out_shape=tuple(jax.ShapeDtypeStruct(a.shape, a.dtype) for a in results),
        in_specs=[anywhere] * 3,
        out_specs=(anywhere,) * 3,
        scratch_shapes=[pltpu.VMEM(a.shape, a.dtype) for a in results] + [dma((2, 3))],
        compiler_params=pltpu.CompilerParams(vmem_limit_bytes=64 * 2**20),
    )(*results)


def solution(mesh):
    in_specs = (
        P("rec", "ctx", None),
        P("rec", "ctx", None),
        P("ctx", None),
        P("ctx", None),
        P("rec", None),
        P("rec", None),
    )
    out_specs = (P("rec", "ctx", None), P("ctx", "rec"), P("ctx", "rec"))
    return jax.shard_map(body, mesh=mesh, in_specs=in_specs, out_specs=out_specs, check_vma=False)
```
